32 devices in a mesh: shots: 2 (over x), gx: 16 (over z, y, core).
Axes of the slice: x: 2, y: 2, z: 4, core: 2. Of those that a mesh axis runs over, the one named last changes fastest.
Arguments:
- velocity: float32 [256, 24, 128], P('gx'), may hold values from 0.05 to 0.18
- source_prior: float32 [512, 24, 128], P(('shots', 'gx')), parts along dimension 0, may hold values from -6 to 6
- source_now: float32 [512, 24, 128], P(('shots', 'gx')), parts along dimension 0, may hold values from -6 to 6
- record_prior: float32 [512, 24, 128], P(('shots', 'gx')), parts along dimension 0, may hold values from -6 to 6
- record_now: float32 [512, 24, 128], P(('shots', 'gx')), parts along dimension 0, may hold values from -6 to 6
- source_inline: int32 [32], P('shots'), parts along dimension 0, may hold values from 0 to 255
- source_crossline: int32 [32], P('shots'), parts along dimension 0, may hold values from 0 to 23
- source_pulse: float32 [32, 2], P('shots'), parts along dimension 0, may hold values from -12 to 12
- receiver_inline: int32 [2048], P('shots'), parts along dimension 0, may hold values from 0 to 255
- receiver_crossline: int32 [2048], P('shots'), parts along dimension 0, may hold values from 0 to 23
- receiver_trace: float32 [2048, 2], P('shots'), parts along dimension 0, may hold values from -12 to 12
- offsets: int32 [17], replicated, may hold values from -8 to 8
Outputs:
- images: bfloat16 [34, 256, 24, 128], P('shots', 'gx'), parts along dimension 0
- adjoint_source: float32 [512, 24, 128], P(('shots', 'gx')), parts along dimension 0
- adjoint_receiver: float32 [512, 24, 128], P(('shots', 'gx')), parts along dimension 0
The draws below stay inside these ranges and needn't reach their ends.
There are 2 independent parts, one for each index of `shots`. The reference program is written for one: setup_inputs(seed, part) draws one part's arguments, and reference() takes and returns one part's arrays. A program takes and returns all parts, laid end to end along the dimension named above; an argument that names none is the same for every part. Nothing has to cross between parts.
All inputs are finite; a program needn't handle non-finite values.
Results may differ from the reference program's by a relative error of at most 0.001.
Values sent between devices are 32-bit elements; how exact they have to be, the bound alone decides.
A program may use at most 128 MiB of HBM per device.

```python
import jax
import jax.numpy as jnp
from jax import lax

NY = 24
NZ = 128
STEPS = 2
NLAG = 17
LAG_MAX = 8
NSRC = 16
NREC = 1024
NX = 256


def with_ends(drawn, key, smallest, top_value):
    longest = drawn.shape.index(max(drawn.shape))
    spots = []
    for shift in (0, 1):
        where = [jax.random.randint(jax.random.fold_in(key, axis), (), 0, length) for axis, length in enumerate(drawn.shape)]
        where[longest] = (where[longest] + shift) % drawn.shape[longest]
        spots.append(tuple(where))
    return drawn.at[spots[0]].set(smallest).at[spots[1]].set(top_value)


def block_levels(rng, dims, split, smallest, top_value):
    def one(axis_at, blocks):
        draws = jax.random.uniform(jax.random.fold_in(jax.random.fold_in(rng, 6), axis_at), (blocks,), jnp.float32, smallest / len(split), top_value / len(split))
        return jnp.repeat(jnp.exp(draws), dims[axis_at] // blocks).reshape((-1,) + (1,) * (len(dims) - axis_at - 1))

    level = one(*split[0])
    for cut in split[1:]:
        level = level * one(*cut)
    return level


def centred(rng, shape, width, limit, pieces=(), held_as=jnp.bfloat16):
    result = width * jax.random.normal(rng, shape, jnp.float32)
    if pieces:
        result = result * block_levels(rng, shape, pieces, -0.22, 0.18)
    return jnp.clip(result, -limit, limit).astype(held_as)


def setup_inputs(seed: int = 0, part: int = 0) -> dict:
    keys = jax.random.split(jax.random.key(seed), 13)
    own_keys = jax.random.split(jax.random.fold_in(keys[12], part), 13)
    velocity = jnp.clip(0.05 + 0.13000001 * jax.random.uniform(keys[0], (NX, NY, NZ), jnp.float32) ** block_levels(keys[0], (NX, NY, NZ), ((0, 16),), -0.2, 0.2), 0.05, 0.18)
    source_prior = centred(own_keys[1], (NX, NY, NZ), 1.0, 6.0, ((0, 16),), jnp.float32)
    source_now = centred(own_keys[2], (NX, NY, NZ), 1.0, 6.0, ((0, 16),), jnp.float32)
    record_prior = centred(own_keys[3], (NX, NY, NZ), 1.0, 6.0, ((0, 16),), jnp.float32)
    record_now = centred(own_keys[4], (NX, NY, NZ), 1.0, 6.0, ((0, 16),), jnp.float32)
    source_inline = with_ends(jax.random.randint(own_keys[5], (NSRC,), 0, NX), jax.random.fold_in(own_keys[5], 1), 0, NX - 1).astype(jnp.int32)
    source_crossline = with_ends(jax.random.randint(own_keys[6], (NSRC,), 0, NY), jax.random.fold_in(own_keys[6], 1), 0, NY - 1).astype(jnp.int32)
    source_pulse = centred(own_keys[7], (NSRC, STEPS), 2.0, 12.0, (), jnp.float32)
    receiver_inline = with_ends(jax.random.randint(own_keys[8], (NREC,), 0, NX), jax.random.fold_in(own_keys[8], 1), 0, NX - 1).astype(jnp.int32)
    receiver_crossline = with_ends(jax.random.randint(own_keys[9], (NREC,), 0, NY), jax.random.fold_in(own_keys[9], 1), 0, NY - 1).astype(jnp.int32)
    receiver_trace = centred(own_keys[10], (NREC, STEPS), 2.0, 12.0, (), jnp.float32)
    offsets = with_ends(jax.random.randint(keys[11], (NLAG,), -LAG_MAX, LAG_MAX + 1), jax.random.fold_in(keys[11], 1), -LAG_MAX, LAG_MAX).astype(jnp.int32)
    return {"velocity": velocity, "source_prior": source_prior, "source_now": source_now, "record_prior": record_prior, "record_now": record_now, "source_inline": source_inline, "source_crossline": source_crossline, "source_pulse": source_pulse, "receiver_inline": receiver_inline, "receiver_crossline": receiver_crossline, "receiver_trace": receiver_trace, "offsets": offsets}


stencil = (-205.0 / 72.0, 8.0 / 5.0, -1.0 / 5.0, 8.0 / 315.0, -1.0 / 560.0)
source_depth = 3
record_depth = 1


def laplace(field):
    cells_x, cells_y, cells_z = field.shape
    padded = jnp.pad(field, 4)
    summed = 3.0 * stencil[0] * field
    for offset in range(1, 5):
        beside_all = padded[4 + offset:4 + offset + cells_x, 4:4 + cells_y, 4:4 + cells_z]
        beside_all = beside_all + padded[4 - offset:4 - offset + cells_x, 4:4 + cells_y, 4:4 + cells_z]
        beside_all = beside_all + padded[4:4 + cells_x, 4 + offset:4 + offset + cells_y, 4:4 + cells_z]
        beside_all = beside_all + padded[4:4 + cells_x, 4 - offset:4 - offset + cells_y, 4:4 + cells_z]
        beside_all = beside_all + padded[4:4 + cells_x, 4:4 + cells_y, 4 + offset:4 + offset + cells_z]
        beside_all = beside_all + padded[4:4 + cells_x, 4:4 + cells_y, 4 - offset:4 - offset + cells_z]
        summed = summed + stencil[offset] * beside_all
    return summed


def injection(place_x, place_y, amplitude, count_x, count_y):
    hits_x = (place_x[:, None] == jnp.arange(count_x, dtype=jnp.int32)[None, :]).astype(jnp.float32) * amplitude[:, None]
    hits_y = (place_y[:, None] == jnp.arange(count_y, dtype=jnp.int32)[None, :]).astype(jnp.float32)
    return jnp.einsum("sx,sy->xy", hits_x, hits_y, precision=lax.Precision.HIGHEST)


def reference(velocity, source_prior, source_now, record_prior, record_now, source_inline, source_crossline, source_pulse, receiver_inline, receiver_crossline, receiver_trace, offsets):
    cells_x, cells_y, cells_z = velocity.shape
    for moment in range(STEPS):
        source_next = 2.0 * source_now - source_prior + velocity * laplace(source_now)
        source_next = source_next.at[:, :, source_depth].add(injection(source_inline, source_crossline, source_pulse[:, moment], cells_x, cells_y))
        record_next = 2.0 * record_now - record_prior + velocity * laplace(record_now)
        record_next = record_next.at[:, :, record_depth].add(injection(receiver_inline, receiver_crossline, receiver_trace[:, moment], cells_x, cells_y))
        source_prior, source_now = source_now, source_next
        record_prior, record_now = record_now, record_next
    wide_source = jnp.pad(source_now, ((LAG_MAX, LAG_MAX), (0, 0), (0, 0)))
    wide_record = jnp.pad(record_now, ((LAG_MAX, LAG_MAX), (0, 0), (0, 0)))

    def single(shift_cells):
        left = lax.dynamic_slice_in_dim(wide_source, (LAG_MAX - shift_cells).astype(jnp.int32), cells_x, 0)
        right = lax.dynamic_slice_in_dim(wide_record, (LAG_MAX + shift_cells).astype(jnp.int32), cells_x, 0)
        return (left * right).astype(jnp.bfloat16)

    images = lax.map(single, offsets)
    squares_source = jnp.pad(source_now * source_now, ((2 * LAG_MAX, 2 * LAG_MAX), (0, 0), (0, 0)))
    squares_record = jnp.pad(record_now * record_now, ((2 * LAG_MAX, 2 * LAG_MAX), (0, 0), (0, 0)))
    weights = (offsets * offsets).astype(jnp.float32) / (LAG_MAX * LAG_MAX * NLAG)

    def accumulate(index, carry):
        toward_source, toward_record = carry
        shift_cells = offsets[index]
        weight = weights[index]
        from_record = lax.dynamic_slice_in_dim(squares_record, (2 * LAG_MAX + 2 * shift_cells).astype(jnp.int32), cells_x, 0)
        from_source = lax.dynamic_slice_in_dim(squares_source, (2 * LAG_MAX - 2 * shift_cells).astype(jnp.int32), cells_x, 0)
        return (toward_source + weight * from_record, toward_record + weight * from_source)

    empty = jnp.zeros(source_now.shape, jnp.float32)
    toward_source, toward_record = lax.fori_loop(0, NLAG, accumulate, (empty, empty))
    return images, source_now * toward_source, record_now * toward_record
```

```python
import functools

import jax
import jax.numpy as jnp
from jax import lax
from jax.experimental import pallas as pl
from jax.experimental.pallas import tpu as pltpu
from jax.sharding import PartitionSpec as P

STEPS = 2
LAG_MAX = 8
REACH = 2 * LAG_MAX
RIM = 4

stencil = (-205.0 / 72.0, 8.0 / 5.0, -1.0 / 5.0, 8.0 / 315.0, -1.0 / 560.0)
depths = (3, 1)
LEFT_PAD = 8


def split_halves(x):
    high = x.astype(jnp.bfloat16)
    low = (x - high.astype(jnp.float32)).astype(jnp.bfloat16)
    return high, low


def depth_band(cells_z):
    rows = lax.broadcasted_iota(jnp.int32, (cells_z, cells_z), 0)
    columns = lax.broadcasted_iota(jnp.int32, (cells_z, cells_z), 1)
    apart = jnp.abs(rows - columns)
    band = jnp.zeros((cells_z, cells_z), jnp.float32)
    for distance in range(1, 5):
        band = jnp.where(apart == distance, stencil[distance], band)
    high, low = split_halves(band)
    return jnp.concatenate([high, high, low], axis=0)


def kernel(
    count,
    velocity,
    source_prior,
    source_now,
    record_prior,
    record_now,
    source_x,
    source_y,
    source_t,
    record_x,
    record_y,
    record_t,
    offsets_row,
    offsets,
    images,
    adjoint_source,
    adjoint_record,
    wide0,
    wide1,
    final,
    padded,
    partial,
    added,
    squares,
    weights,
    send0,
    recv0,
    send1,
    recv1,
    send2,
    recv2,
):
    extent, cells_y, cells_z = velocity.shape
    lags = images.shape[0]
    me = lax.axis_index("gx")
    has_lower = me > 0
    has_upper = me < count - 1
    lower = jnp.maximum(me - 1, 0)
    upper = jnp.minimum(me + 1, count - 1)
    nows = (source_now, record_now)
    priors = (source_prior, record_prior)

    def copy(src, dst, send, recv, device):
        return pltpu.make_async_remote_copy(
            src_ref=src,
            dst_ref=dst,
            send_sem=send,
            recv_sem=recv,
            device_id={"gx": device},
            device_id_type=pl.DeviceIdType.MESH,
        )

    down, up = [], []
    for f in range(2):
        down.append(copy(nows[f].at[pl.ds(0, RIM)], wide0.at[f, pl.ds(RIM + extent, RIM)], send0.at[f], recv0.at[f], lower))
        up.append(copy(nows[f].at[pl.ds(extent - RIM, RIM)], wide0.at[f, pl.ds(0, RIM)], send0.at[2 + f], recv0.at[2 + f], upper))
    first = (down, up)
    second = (
        [copy(wide1.at[:, pl.ds(RIM, RIM)], wide1.at[:, pl.ds(RIM + extent, RIM)], send1.at[0], recv1.at[0], lower)],
        [copy(wide1.at[:, pl.ds(extent, RIM)], wide1.at[:, pl.ds(0, RIM)], send1.at[1], recv1.at[1], upper)],
    )

    def final_copies(start, length, slot):
        src = final.at[:, pl.ds(REACH + start, length)]
        return (
            copy(src, final.at[:, pl.ds(REACH + extent + start, length)], send2.at[slot], recv2.at[slot], lower),
            copy(src, final.at[:, pl.ds(REACH - extent + start, length)], send2.at[3 + slot], recv2.at[3 + slot], upper),
        )

    pieces = ((RIM, extent - 2 * RIM), (0, RIM), (extent - RIM, RIM))
    third = [final_copies(start, length, slot) for slot, (start, length) in enumerate(pieces)]

    def start(group):
        @pl.when(has_lower)
        def _():
            for one in group[0]:
                one.start()

        @pl.when(has_upper)
        def _():
            for one in group[1]:
                one.start()

    def arrive(group):
        @pl.when(has_upper)
        def _():
            for one in group[0]:
                one.wait_recv()

        @pl.when(has_lower)
        def _():
            for one in group[1]:
                one.wait_recv()

    def leave(group):
        @pl.when(has_lower)
        def _():
            for one in group[0]:
                one.wait_send()

        @pl.when(has_upper)
        def _():
            for one in group[1]:
                one.wait_send()

    barrier = pltpu.get_barrier_semaphore()

    @pl.when(has_lower)
    def _():
        pl.semaphore_signal(barrier, inc=1, device_id={"gx": lower}, device_id_type=pl.DeviceIdType.MESH)

    @pl.when(has_upper)
    def _():
        pl.semaphore_signal(barrier, inc=1, device_id={"gx": upper}, device_id_type=pl.DeviceIdType.MESH)

    @pl.when(jnp.logical_not(has_lower))
    def _():
        wide0[:, pl.ds(0, RIM)] = jnp.zeros((2, RIM, cells_y, cells_z), jnp.float32)
        wide1[:, pl.ds(0, RIM)] = jnp.zeros((2, RIM, cells_y, cells_z), jnp.float32)
        final[:, pl.ds(0, REACH)] = jnp.zeros((2, REACH, cells_y, cells_z), jnp.float32)

    @pl.when(jnp.logical_not(has_upper))
    def _():
        wide0[:, pl.ds(RIM + extent, RIM)] = jnp.zeros((2, RIM, cells_y, cells_z), jnp.float32)
        wide1[:, pl.ds(RIM + extent, RIM)] = jnp.zeros((2, RIM, cells_y, cells_z), jnp.float32)
        final[:, pl.ds(REACH + extent, REACH)] = jnp.zeros((2, REACH, cells_y, cells_z), jnp.float32)

    pl.semaphore_wait(barrier, has_lower.astype(jnp.int32) + has_upper.astype(jnp.int32))

    start(first)

    padded[:, :, pl.ds(0, LEFT_PAD)] = jnp.zeros((2, extent, LEFT_PAD, cells_z), jnp.float32)
    padded[:, :, pl.ds(LEFT_PAD + cells_y, LEFT_PAD)] = jnp.zeros((2, extent, LEFT_PAD, cells_z), jnp.float32)
    for f in range(2):
        wide0[f, pl.ds(RIM, extent)] = nows[f][...]
        padded[f, :, pl.ds(LEFT_PAD, cells_y)] = nows[f][...]

    rows = extent * cells_y
    for f, (place_x, place_y, pulse) in enumerate(((source_x, source_y, source_t), (record_x, record_y, record_t))):
        number = place_x.shape[1]
        cell = (place_x[...] - me * extent) * cells_y + place_y[...]
        hits = jnp.where(lax.broadcasted_iota(jnp.int32, (rows, number), 0) == cell, 1.0, 0.0).astype(jnp.bfloat16)
        line = lax.broadcasted_iota(jnp.int32, (STEPS * cells_z, number), 0)
        spread = jnp.zeros((STEPS * cells_z, number), jnp.float32)
        for moment in range(STEPS):
            spread = jnp.where(line == moment * cells_z + depths[f], pulse[pl.ds(moment, 1), :], spread)
        plane = jnp.zeros((rows, STEPS * cells_z), jnp.float32)
        for part in split_halves(spread):
            plane = plane + lax.dot_general(hits, part, (((1,), (1,)), ((), ())), preferred_element_type=jnp.float32)
        for moment in range(STEPS):
            added[moment, f] = plane[:, moment * cells_z : (moment + 1) * cells_z].reshape(extent, cells_y, cells_z)

    band = depth_band(cells_z)

    def beside(moment, wide, before):
        for f in range(2):
            flat = wide[f, pl.ds(RIM, extent)].reshape(rows, cells_z)
            high, low = split_halves(flat)
            along = jnp.dot(jnp.concatenate([high, low, high], axis=1), band, preferred_element_type=jnp.float32)
            along = along.reshape(extent, cells_y, cells_z)
            for x in range(0, extent, RIM):
                centre = wide[f, pl.ds(RIM + x, RIM)]
                total = 3.0 * stencil[0] * centre + along[x : x + RIM]
                for distance in range(1, 5):
                    pair = padded[f, pl.ds(x, RIM), pl.ds(LEFT_PAD - distance, cells_y)] + padded[f, pl.ds(x, RIM), pl.ds(LEFT_PAD + distance, cells_y)]
                    total = total + stencil[distance] * pair
                partial[f, pl.ds(x, RIM)] = (
                    2.0 * centre - before(f, x) + velocity[pl.ds(x, RIM)] * total + added[moment, f, pl.ds(x, RIM)]
                )

    def finished(wide, f, x):
        total = None
        for distance in range(1, 5):
            pair = wide[f, pl.ds(RIM + x - distance, RIM)] + wide[f, pl.ds(RIM + x + distance, RIM)]
            term = stencil[distance] * pair
            total = term if total is None else total + term
        return partial[f, pl.ds(x, RIM)] + velocity[pl.ds(x, RIM)] * total

    inner = range(RIM, extent - RIM, RIM)
    edges = (0, extent - RIM)

    def keep_first(f, x):
        value = finished(wide0, f, x)
        wide1[f, pl.ds(RIM + x, RIM)] = value
        padded[f, pl.ds(x, RIM), pl.ds(LEFT_PAD, cells_y)] = value

    def keep_final(f, x):
        value = finished(wide1, f, x)
        final[f, pl.ds(REACH + x, RIM)] = value
        squares[f, pl.ds(REACH + x, RIM)] = value * value

    beside(0, wide0, lambda f, x: priors[f][pl.ds(x, RIM)])
    for f in range(2):
        for x in inner:
            keep_first(f, x)
    arrive(first)
    for f in range(2):
        for x in edges:
            keep_first(f, x)
    start(second)

    beside(1, wide1, lambda f, x: wide0[f, pl.ds(RIM + x, RIM)])
    for f in range(2):
        for x in inner:
            keep_final(f, x)
    start(([third[0][0]], [third[0][1]]))
    arrive(second)
    for f in range(2):
        for x in edges:
            keep_final(f, x)
    start(([third[1][0], third[2][0]], [third[2][1], third[1][1]]))

    signed = lax.broadcasted_iota(jnp.int32, (2 * LAG_MAX + 1, lags), 0) - LAG_MAX
    same = jnp.where(signed == offsets_row[...], 1.0, 0.0)
    tally = jnp.sum(same, axis=1, keepdims=True)
    signed_column = lax.broadcasted_iota(jnp.int32, (2 * LAG_MAX + 1, cells_z), 0) - LAG_MAX
    weight = (signed_column * signed_column).astype(jnp.float32) / (LAG_MAX * LAG_MAX * lags)
    weights[pl.ds(0, 2 * LAG_MAX + 1), :] = weight * tally

    arrive(([one[0] for one in third], [one[1] for one in third]))

    def picture(k, carry):
        shift = offsets[k]
        left = final[0, pl.ds(REACH - shift, extent)]
        right = final[1, pl.ds(REACH + shift, extent)]
        images[k] = (left * right).astype(jnp.bfloat16)
        return carry

    lax.fori_loop(0, lags, picture, 0)

    for f in range(2):
        for side in (0, REACH + extent):
            value = final[f, pl.ds(side, REACH)]
            squares[f, pl.ds(side, REACH)] = value * value
    for f, out in ((0, adjoint_source), (1, adjoint_record)):
        sign = 2 if f == 0 else -2
        for x in range(0, extent, RIM):
            total = None
            for lag in range(-LAG_MAX, LAG_MAX + 1):
                if lag == 0:
                    continue
                term = weights[pl.ds(lag + LAG_MAX, 1), :] * squares[1 - f, pl.ds(REACH + x + sign * lag, RIM)]
                total = term if total is None else total + term
            out[pl.ds(x, RIM)] = final[f, pl.ds(REACH + x, RIM)] * total

    leave(first)
    leave(second)
    leave(([one[0] for one in third], [one[1] for one in third]))


def per_device(
    velocity,
    source_prior,
    source_now,
    record_prior,
    record_now,
    source_inline,
    source_crossline,
    source_pulse,
    receiver_inline,
    receiver_crossline,
    receiver_trace,
    offsets,
):
    extent, cells_y, cells_z = velocity.shape
    lags = offsets.shape[0]
    field = jax.ShapeDtypeStruct(velocity.shape, jnp.float32)
    vmem = pl.BlockSpec(memory_space=pltpu.VMEM)
    smem = pl.BlockSpec(memory_space=pltpu.SMEM)
    call = pl.pallas_call(
        functools.partial(kernel, lax.axis_size("gx")),
        out_shape=(jax.ShapeDtypeStruct((lags,) + velocity.shape, jnp.bfloat16), field, field),
        in_specs=[vmem] * 12 + [smem],
        out_specs=(vmem, vmem, vmem),
        scratch_shapes=[
            pltpu.VMEM((2, extent + 2 * RIM, cells_y, cells_z), jnp.float32),
            pltpu.VMEM((2, extent + 2 * RIM, cells_y, cells_z), jnp.float32),
            pltpu.VMEM((2, extent + 2 * REACH, cells_y, cells_z), jnp.float32),
            pltpu.VMEM((2, extent, cells_y + 2 * LEFT_PAD, cells_z), jnp.float32),
            pltpu.VMEM((2, extent, cells_y, cells_z), jnp.float32),
            pltpu.VMEM((STEPS, 2, extent, cells_y, cells_z), jnp.float32),
            pltpu.VMEM((2, extent + 2 * REACH, cells_y, cells_z), jnp.float32),
            pltpu.VMEM((2 * LAG_MAX + 8, cells_z), jnp.float32),
            pltpu.SemaphoreType.DMA((4,)),
            pltpu.SemaphoreType.DMA((4,)),
            pltpu.SemaphoreType.DMA((2,)),
            pltpu.SemaphoreType.DMA((2,)),
            pltpu.SemaphoreType.DMA((6,)),
            pltpu.SemaphoreType.DMA((6,)),
        ],
        compiler_params=pltpu.CompilerParams(
            collective_id=0, has_side_effects=True, vmem_limit_bytes=40 * 1024 * 1024
        ),
    )
    return call(
        velocity,
        source_prior,
        source_now,
        record_prior,
        record_now,
        source_inline.reshape(1, -1),
        source_crossline.reshape(1, -1),
        source_pulse.T,
        receiver_inline.reshape(1, -1),
        receiver_crossline.reshape(1, -1),
        receiver_trace.T,
        offsets.reshape(1, -1),
        offsets,
    )


def solution(mesh):
    in_specs = (
        P("gx", None, None),
        P(("shots", "gx"), None, None),
        P(("shots", "gx"), None, None),
        P(("shots", "gx"), None, None),
        P(("shots", "gx"), None, None),
        P("shots"),
        P("shots"),
        P("shots", None),
        P("shots"),
        P("shots"),
        P("shots", None),
        P(),
    )
    out_specs = (
        P("shots", "gx", None, None),
        P(("shots", "gx"), None, None),
        P(("shots", "gx"), None, None),
    )
    return jax.shard_map(
        per_device, mesh=mesh, in_specs=in_specs, out_specs=out_specs, check_vma=False
    )
```

```python
import functools

import jax
import jax.numpy as jnp
from jax import lax
from jax.experimental import pallas as pl
from jax.experimental.pallas import tpu as pltpu
from jax.sharding import PartitionSpec as P

STEPS = 2
LAG_MAX = 8
REACH = 2 * LAG_MAX
RIM = 4

stencil = (-205.0 / 72.0, 8.0 / 5.0, -1.0 / 5.0, 8.0 / 315.0, -1.0 / 560.0)
depths = (3, 1)
LEFT_PAD = 8


def split_halves(x):
    high = x.astype(jnp.bfloat16)
    low = (x - high.astype(jnp.float32)).astype(jnp.bfloat16)
    return high, low


def depth_band(cells_z):
    rows = lax.broadcasted_iota(jnp.int32, (cells_z, cells_z), 0)
    columns = lax.broadcasted_iota(jnp.int32, (cells_z, cells_z), 1)
    apart = jnp.abs(rows - columns)
    band = jnp.zeros((cells_z, cells_z), jnp.float32)
    for distance in range(1, 5):
        band = jnp.where(apart == distance, stencil[distance], band)
    high, low = split_halves(band)
    return jnp.concatenate([high, high, low], axis=0)


def kernel(
    count,
    velocity_hbm,
    source_prior,
    source_now,
    record_prior,
    record_now,
    source_x_hbm,
    source_y_hbm,
    source_t_hbm,
    record_x_hbm,
    record_y_hbm,
    record_t_hbm,
    offsets_row_hbm,
    offsets_hbm,
    images,
    adjoint_source,
    adjoint_record,
    wide0,
    wide1,
    final,
    padded,
    partial,
    added,
    squares,
    weights,
    send0,
    recv0,
    send1,
    recv1,
    send2,
    recv2,
    velocity,
    prior,
    source_x,
    source_y,
    source_t,
    record_x,
    record_y,
    record_t,
    offsets_row,
    offsets,
    loaded,
):
    extent, cells_y, cells_z = velocity.shape
    lags = images.shape[0]
    small = [
        pltpu.make_async_copy(src, dst, loaded.at[slot])
        for slot, (src, dst) in enumerate((
            (record_x_hbm, record_x),
            (record_y_hbm, record_y),
            (record_t_hbm, record_t),
            (source_x_hbm, source_x),
            (source_y_hbm, source_y),
            (source_t_hbm, source_t),
            (offsets_row_hbm, offsets_row),
            (offsets_hbm, offsets),
        ))
    ]
    me = lax.axis_index("gx")
    has_lower = me > 0
    has_upper = me < count - 1
    lower = jnp.maximum(me - 1, 0)
    upper = jnp.minimum(me + 1, count - 1)
    nows = (source_now, record_now)
    priors = (source_prior, record_prior)

    def copy(src, dst, send, recv, device):
        return pltpu.make_async_remote_copy(
            src_ref=src,
            dst_ref=dst,
            send_sem=send,
            recv_sem=recv,
            device_id={"gx": device},
            device_id_type=pl.DeviceIdType.MESH,
        )

    down, up = [], []
    for f in range(2):
        down.append(copy(nows[f].at[pl.ds(0, RIM)], wide0.at[f, pl.ds(RIM + extent, RIM)], send0.at[f], recv0.at[f], lower))
        up.append(copy(nows[f].at[pl.ds(extent - RIM, RIM)], wide0.at[f, pl.ds(0, RIM)], send0.at[2 + f], recv0.at[2 + f], upper))
    first = (down, up)
    second = (
        [copy(wide1.at[:, pl.ds(RIM, RIM)], wide1.at[:, pl.ds(RIM + extent, RIM)], send1.at[0], recv1.at[0], lower)],
        [copy(wide1.at[:, pl.ds(extent, RIM)], wide1.at[:, pl.ds(0, RIM)], send1.at[1], recv1.at[1], upper)],
    )

    def final_copies(start, length, slot):
        src = final.at[:, pl.ds(REACH + start, length)]
        return (
            copy(src, final.at[:, pl.ds(REACH + extent + start, length)], send2.at[slot], recv2.at[slot], lower),
            copy(src, final.at[:, pl.ds(REACH - extent + start, length)], send2.at[3 + slot], recv2.at[3 + slot], upper),
        )

    pieces = ((RIM, extent - 2 * RIM), (0, RIM), (extent - RIM, RIM))
    third = [final_copies(start, length, slot) for slot, (start, length) in enumerate(pieces)]

    def start(group):
        @pl.when(has_lower)
        def _():
            for one in group[0]:
                one.start()

        @pl.when(has_upper)
        def _():
            for one in group[1]:
                one.start()

    def arrive(group):
        @pl.when(has_upper)
        def _():
            for one in group[0]:
                one.wait_recv()

        @pl.when(has_lower)
        def _():
            for one in group[1]:
                one.wait_recv()

    def leave(group):
        @pl.when(has_lower)
        def _():
            for one in group[0]:
                one.wait_send()

        @pl.when(has_upper)
        def _():
            for one in group[1]:
                one.wait_send()

    large = []
    for f in range(2):
        large.append((nows[f], wide0.at[f, pl.ds(RIM, extent)]))
        large.append((nows[f], padded.at[f, :, pl.ds(LEFT_PAD, cells_y)]))
        large.append((priors[f], prior.at[f]))
    large.append((velocity_hbm, velocity))
    large = [
        pltpu.make_async_copy(src, dst, loaded.at[len(small) + slot])
        for slot, (src, dst) in enumerate(large)
    ]

    barrier = pltpu.get_barrier_semaphore()

    @pl.when(has_lower)
    def _():
        pl.semaphore_signal(barrier, inc=1, device_id={"gx": lower}, device_id_type=pl.DeviceIdType.MESH)

    @pl.when(has_upper)
    def _():
        pl.semaphore_signal(barrier, inc=1, device_id={"gx": upper}, device_id_type=pl.DeviceIdType.MESH)

    for one in small + large:
        one.start()

    @pl.when(jnp.logical_not(has_lower))
    def _():
        wide0[:, pl.ds(0, RIM)] = jnp.zeros((2, RIM, cells_y, cells_z), jnp.float32)
        wide1[:, pl.ds(0, RIM)] = jnp.zeros((2, RIM, cells_y, cells_z), jnp.float32)
        final[:, pl.ds(0, REACH)] = jnp.zeros((2, REACH, cells_y, cells_z), jnp.float32)

    @pl.when(jnp.logical_not(has_upper))
    def _():
        wide0[:, pl.ds(RIM + extent, RIM)] = jnp.zeros((2, RIM, cells_y, cells_z), jnp.float32)
        wide1[:, pl.ds(RIM + extent, RIM)] = jnp.zeros((2, RIM, cells_y, cells_z), jnp.float32)
        final[:, pl.ds(REACH + extent, REACH)] = jnp.zeros((2, REACH, cells_y, cells_z), jnp.float32)

    pl.semaphore_wait(barrier, has_lower.astype(jnp.int32) + has_upper.astype(jnp.int32))

    start(first)

    padded[:, :, pl.ds(0, LEFT_PAD)] = jnp.zeros((2, extent, LEFT_PAD, cells_z), jnp.float32)
    padded[:, :, pl.ds(LEFT_PAD + cells_y, LEFT_PAD)] = jnp.zeros((2, extent, LEFT_PAD, cells_z), jnp.float32)
    for one in small:
        one.wait()

    rows = extent * cells_y
    for f, (place_x, place_y, pulse) in enumerate(((source_x, source_y, source_t), (record_x, record_y, record_t))):
        number = place_x.shape[1]
        cell = (place_x[...] - me * extent) * cells_y + place_y[...]
        hits = jnp.where(lax.broadcasted_iota(jnp.int32, (rows, number), 0) == cell, 1.0, 0.0).astype(jnp.bfloat16)
        line = lax.broadcasted_iota(jnp.int32, (STEPS * cells_z, number), 0)
        spread = jnp.zeros((STEPS * cells_z, number), jnp.float32)
        for moment in range(STEPS):
            spread = jnp.where(line == moment * cells_z + depths[f], pulse[pl.ds(moment, 1), :], spread)
        plane = jnp.zeros((rows, STEPS * cells_z), jnp.float32)
        for part in split_halves(spread):
            plane = plane + lax.dot_general(hits, part, (((1,), (1,)), ((), ())), preferred_element_type=jnp.float32)
        for moment in range(STEPS):
            added[moment, f] = plane[:, moment * cells_z : (moment + 1) * cells_z].reshape(extent, cells_y, cells_z)

    band = depth_band(cells_z)

    def beside(moment, wide, before):
        for f in range(2):
            flat = wide[f, pl.ds(RIM, extent)].reshape(rows, cells_z)
            high, low = split_halves(flat)
            along = jnp.dot(jnp.concatenate([high, low, high], axis=1), band, preferred_element_type=jnp.float32)
            along = along.reshape(extent, cells_y, cells_z)
            for x in range(0, extent, RIM):
                centre = wide[f, pl.ds(RIM + x, RIM)]
                total = 3.0 * stencil[0] * centre + along[x : x + RIM]
                for distance in range(1, 5):
                    pair = padded[f, pl.ds(x, RIM), pl.ds(LEFT_PAD - distance, cells_y)] + padded[f, pl.ds(x, RIM), pl.ds(LEFT_PAD + distance, cells_y)]
                    total = total + stencil[distance] * pair
                partial[f, pl.ds(x, RIM)] = (
                    2.0 * centre - before(f, x) + velocity[pl.ds(x, RIM)] * total + added[moment, f, pl.ds(x, RIM)]
                )

    def finished(wide, f, x):
        total = None
        for distance in range(1, 5):
            pair = wide[f, pl.ds(RIM + x - distance, RIM)] + wide[f, pl.ds(RIM + x + distance, RIM)]
            term = stencil[distance] * pair
            total = term if total is None else total + term
        return partial[f, pl.ds(x, RIM)] + velocity[pl.ds(x, RIM)] * total

    inner = range(RIM, extent - RIM, RIM)
    edges = (0, extent - RIM)

    def keep_first(f, x):
        value = finished(wide0, f, x)
        wide1[f, pl.ds(RIM + x, RIM)] = value
        padded[f, pl.ds(x, RIM), pl.ds(LEFT_PAD, cells_y)] = value

    def keep_final(f, x):
        value = finished(wide1, f, x)
        final[f, pl.ds(REACH + x, RIM)] = value
        squares[f, pl.ds(REACH + x, RIM)] = value * value

    for one in large:
        one.wait()
    beside(0, wide0, lambda f, x: prior[f, pl.ds(x, RIM)])
    for f in range(2):
        for x in inner:
            keep_first(f, x)
    arrive(first)
    for f in range(2):
        for x in edges:
            keep_first(f, x)
    start(second)

    beside(1, wide1, lambda f, x: wide0[f, pl.ds(RIM + x, RIM)])
    for f in range(2):
        for x in inner:
            keep_final(f, x)
    start(([third[0][0]], [third[0][1]]))
    arrive(second)
    for f in range(2):
        for x in edges:
            keep_final(f, x)
    start(([third[1][0], third[2][0]], [third[2][1], third[1][1]]))

    signed = lax.broadcasted_iota(jnp.int32, (2 * LAG_MAX + 1, lags), 0) - LAG_MAX
    same = jnp.where(signed == offsets_row[...], 1.0, 0.0)
    tally = jnp.sum(same, axis=1, keepdims=True)
    signed_column = lax.broadcasted_iota(jnp.int32, (2 * LAG_MAX + 1, cells_z), 0) - LAG_MAX
    weight = (signed_column * signed_column).astype(jnp.float32) / (LAG_MAX * LAG_MAX * lags)
    weights[pl.ds(0, 2 * LAG_MAX + 1), :] = weight * tally

    arrive(([one[0] for one in third], [one[1] for one in third]))

    def picture(k, carry):
        shift = offsets[k]
        left = final[0, pl.ds(REACH - shift, extent)]
        right = final[1, pl.ds(REACH + shift, extent)]
        images[k] = (left * right).astype(jnp.bfloat16)
        return carry

    lax.fori_loop(0, lags, picture, 0)

    for f in range(2):
        for side in (0, REACH + extent):
            value = final[f, pl.ds(side, REACH)]
            squares[f, pl.ds(side, REACH)] = value * value
    for f, out in ((0, adjoint_source), (1, adjoint_record)):
        sign = 2 if f == 0 else -2
        for x in range(0, extent, RIM):
            total = None
            for lag in range(-LAG_MAX, LAG_MAX + 1):
                if lag == 0:
                    continue
                term = weights[pl.ds(lag + LAG_MAX, 1), :] * squares[1 - f, pl.ds(REACH + x + sign * lag, RIM)]
                total = term if total is None else total + term
            out[pl.ds(x, RIM)] = final[f, pl.ds(REACH + x, RIM)] * total

    leave(first)
    leave(second)
    leave(([one[0] for one in third], [one[1] for one in third]))


def write_out(*refs):
    count = (len(refs) - 1) // 2
    copies = [pltpu.make_async_copy(refs[i], refs[count + i], refs[-1].at[i]) for i in range(count)]
    for one in copies:
        one.start()
    for one in copies:
        one.wait()


def per_device(
    velocity,
    source_prior,
    source_now,
    record_prior,
    record_now,
    source_inline,
    source_crossline,
    source_pulse,
    receiver_inline,
    receiver_crossline,
    receiver_trace,
    offsets,
):
    extent, cells_y, cells_z = velocity.shape
    lags = offsets.shape[0]
    field = jax.ShapeDtypeStruct(velocity.shape, jnp.float32)
    vmem = pl.BlockSpec(memory_space=pltpu.VMEM)
    hbm = pl.BlockSpec(memory_space=pltpu.HBM)
    shapes = (jax.ShapeDtypeStruct((lags,) + velocity.shape, jnp.bfloat16), field, field)
    sources, receivers = source_inline.shape[0], receiver_inline.shape[0]
    call = pl.pallas_call(
        functools.partial(kernel, lax.axis_size("gx")),
        out_shape=shapes,
        in_specs=[hbm] * 13,
        out_specs=(vmem, vmem, vmem),
        scratch_shapes=[
            pltpu.VMEM((2, extent + 2 * RIM, cells_y, cells_z), jnp.float32),
            pltpu.VMEM((2, extent + 2 * RIM, cells_y, cells_z), jnp.float32),
            pltpu.VMEM((2, extent + 2 * REACH, cells_y, cells_z), jnp.float32),
            pltpu.VMEM((2, extent, cells_y + 2 * LEFT_PAD, cells_z), jnp.float32),
            pltpu.VMEM((2, extent, cells_y, cells_z), jnp.float32),
            pltpu.VMEM((STEPS, 2, extent, cells_y, cells_z), jnp.float32),
            pltpu.VMEM((2, extent + 2 * REACH, cells_y, cells_z), jnp.float32),
            pltpu.VMEM((2 * LAG_MAX + 8, cells_z), jnp.float32),
            pltpu.SemaphoreType.DMA((4,)),
            pltpu.SemaphoreType.DMA((4,)),
            pltpu.SemaphoreType.DMA((2,)),
            pltpu.SemaphoreType.DMA((2,)),
            pltpu.SemaphoreType.DMA((6,)),
            pltpu.SemaphoreType.DMA((6,)),
            pltpu.VMEM(velocity.shape, jnp.float32),
            pltpu.VMEM((2,) + velocity.shape, jnp.float32),
            pltpu.VMEM((1, sources), jnp.int32),
            pltpu.VMEM((1, sources), jnp.int32),
            pltpu.VMEM((STEPS, sources), jnp.float32),
            pltpu.VMEM((1, receivers), jnp.int32),
            pltpu.VMEM((1, receivers), jnp.int32),
            pltpu.VMEM((STEPS, receivers), jnp.float32),
            pltpu.VMEM((1, lags), jnp.int32),
            pltpu.SMEM((lags,), jnp.int32),
            pltpu.SemaphoreType.DMA((15,)),
        ],
        compiler_params=pltpu.CompilerParams(
            collective_id=0, has_side_effects=True, vmem_limit_bytes=40 * 1024 * 1024
        ),
    )
    operands = (
        velocity,
        source_prior,
        source_now,
        record_prior,
        record_now,
        source_inline.reshape(1, -1),
        source_crossline.reshape(1, -1),
        source_pulse.T,
        receiver_inline.reshape(1, -1),
        receiver_crossline.reshape(1, -1),
        receiver_trace.T,
        offsets.reshape(1, -1),
        offsets,
    )
    held = call(*[pltpu.with_memory_space_constraint(one, pltpu.HBM) for one in operands])
    return pl.pallas_call(
        write_out,
        out_shape=shapes,
        in_specs=[vmem] * len(shapes),
        out_specs=(hbm,) * len(shapes),
        scratch_shapes=[pltpu.SemaphoreType.DMA((len(shapes),))],
        compiler_params=pltpu.CompilerParams(vmem_limit_bytes=4 * 1024 * 1024),
    )(*held)


def solution(mesh):
    in_specs = (
        P("gx", None, None),
        P(("shots", "gx"), None, None),
        P(("shots", "gx"), None, None),
        P(("shots", "gx"), None, None),
        P(("shots", "gx"), None, None),
        P("shots"),
        P("shots"),
        P("shots", None),
        P("shots"),
        P("shots"),
        P("shots", None),
        P(),
    )
    out_specs = (
        P("shots", "gx", None, None),
        P(("shots", "gx"), None, None),
        P(("shots", "gx"), None, None),
    )
    return jax.shard_map(
        per_device, mesh=mesh, in_specs=in_specs, out_specs=out_specs, check_vma=False
    )
```

```python
import functools

import jax
import jax.numpy as jnp
from jax import lax
from jax.experimental import pallas as pl
from jax.experimental.pallas import tpu as pltpu
from jax.sharding import PartitionSpec as P

STEPS = 2
LAG_MAX = 8
REACH = 2 * LAG_MAX
RIM = 4

stencil = (-205.0 / 72.0, 8.0 / 5.0, -1.0 / 5.0, 8.0 / 315.0, -1.0 / 560.0)
depths = (3, 1)
LEFT_PAD = 8


def split_halves(x):
    high = x.astype(jnp.bfloat16)
    low = (x - high.astype(jnp.float32)).astype(jnp.bfloat16)
    return high, low


def depth_band(cells_z):
    rows = lax.broadcasted_iota(jnp.int32, (cells_z, cells_z), 0)
    columns = lax.broadcasted_iota(jnp.int32, (cells_z, cells_z), 1)
    apart = jnp.abs(rows - columns)
    band = jnp.zeros((cells_z, cells_z), jnp.float32)
    for distance in range(1, 5):
        band = jnp.where(apart == distance, stencil[distance], band)
    high, low = split_halves(band)
    return jnp.concatenate([high, high, low], axis=0)


def kernel(
    count,
    velocity_hbm,
    source_prior,
    source_now,
    record_prior,
    record_now,
    source_x_hbm,
    source_y_hbm,
    source_t_hbm,
    record_x_hbm,
    record_y_hbm,
    record_t_hbm,
    offsets_row_hbm,
    offsets_hbm,
    images,
    adjoint_source,
    adjoint_record,
    wide0,
    wide1,
    near,
    far_low,
    far_high,
    padded,
    partial,
    added,
    squares,
    weights,
    send0,
    recv0,
    send1,
    recv1,
    send2,
    recv2,
    velocity,
    prior,
    source_x,
    source_y,
    source_t,
    record_x,
    record_y,
    record_t,
    offsets_row,
    offsets,
    loaded,
):
    extent, cells_y, cells_z = velocity.shape
    lags = images.shape[0]
    small = [
        pltpu.make_async_copy(src, dst, loaded.at[slot])
        for slot, (src, dst) in enumerate((
            (record_x_hbm, record_x),
            (record_y_hbm, record_y),
            (record_t_hbm, record_t),
            (source_x_hbm, source_x),
            (source_y_hbm, source_y),
            (source_t_hbm, source_t),
            (offsets_row_hbm, offsets_row),
            (offsets_hbm, offsets),
        ))
    ]
    me = lax.axis_index("gx")
    has_lower = me > 0
    has_upper = me < count - 1
    lower = jnp.maximum(me - 1, 0)
    upper = jnp.minimum(me + 1, count - 1)
    nows = (source_now, record_now)
    priors = (source_prior, record_prior)

    def copy(src, dst, send, recv, device):
        return pltpu.make_async_remote_copy(
            src_ref=src,
            dst_ref=dst,
            send_sem=send,
            recv_sem=recv,
            device_id={"gx": device},
            device_id_type=pl.DeviceIdType.MESH,
        )

    down, up = [], []
    for f in range(2):
        down.append(copy(nows[f].at[pl.ds(0, RIM)], wide0.at[f, pl.ds(RIM + extent, RIM)], send0.at[f], recv0.at[f], lower))
        up.append(copy(nows[f].at[pl.ds(extent - RIM, RIM)], wide0.at[f, pl.ds(0, RIM)], send0.at[2 + f], recv0.at[2 + f], upper))
    first = (down, up)
    second = (
        [copy(wide1.at[:, pl.ds(RIM, RIM)], wide1.at[:, pl.ds(RIM + extent, RIM)], send1.at[0], recv1.at[0], lower)],
        [copy(wide1.at[:, pl.ds(extent, RIM)], wide1.at[:, pl.ds(0, RIM)], send1.at[1], recv1.at[1], upper)],
    )

    def final_copies(slot, to_lower, length):
        shared = send2.at[slot], recv2.at[slot]
        opposite = extent - to_lower - length

        def target(first_cell, low_side):
            if low_side:
                if first_cell >= extent - LAG_MAX:
                    return near.at[:, pl.ds(first_cell - extent + LAG_MAX, length)]
                return far_low.at[:, pl.ds(first_cell, length)]
            if first_cell < LAG_MAX:
                return near.at[:, pl.ds(LAG_MAX + extent + first_cell, length)]
            return far_high.at[:, pl.ds(first_cell - LAG_MAX, length)]

        return (
            [copy(near.at[:, pl.ds(LAG_MAX + to_lower, length)], target(to_lower, False), *shared, lower)],
            [copy(near.at[:, pl.ds(LAG_MAX + opposite, length)], target(opposite, True), send2.at[4 + slot], recv2.at[4 + slot], upper)],
        )

    near_early = final_copies(0, RIM, LAG_MAX - RIM)
    far_early = final_copies(1, LAG_MAX, extent - RIM - LAG_MAX)
    near_late = final_copies(2, 0, RIM)
    far_late = final_copies(3, extent - RIM, RIM)

    def start(group):
        @pl.when(has_lower)
        def _():
            for one in group[0]:
                one.start()

        @pl.when(has_upper)
        def _():
            for one in group[1]:
                one.start()

    def arrive(group):
        @pl.when(has_upper)
        def _():
            for one in group[0]:
                one.wait_recv()

        @pl.when(has_lower)
        def _():
            for one in group[1]:
                one.wait_recv()

    def leave(group):
        @pl.when(has_lower)
        def _():
            for one in group[0]:
                one.wait_send()

        @pl.when(has_upper)
        def _():
            for one in group[1]:
                one.wait_send()

    large = []
    for f in range(2):
        large.append((nows[f], wide0.at[f, pl.ds(RIM, extent)]))
        large.append((nows[f], padded.at[f, :, pl.ds(LEFT_PAD, cells_y)]))
        large.append((priors[f], prior.at[f]))
    large.append((velocity_hbm, velocity))
    large = [
        pltpu.make_async_copy(src, dst, loaded.at[len(small) + slot])
        for slot, (src, dst) in enumerate(large)
    ]

    barrier = pltpu.get_barrier_semaphore()

    @pl.when(has_lower)
    def _():
        pl.semaphore_signal(barrier, inc=1, device_id={"gx": lower}, device_id_type=pl.DeviceIdType.MESH)

    @pl.when(has_upper)
    def _():
        pl.semaphore_signal(barrier, inc=1, device_id={"gx": upper}, device_id_type=pl.DeviceIdType.MESH)

    for one in small + large:
        one.start()

    @pl.when(jnp.logical_not(has_lower))
    def _():
        wide0[:, pl.ds(0, RIM)] = jnp.zeros((2, RIM, cells_y, cells_z), jnp.float32)
        wide1[:, pl.ds(0, RIM)] = jnp.zeros((2, RIM, cells_y, cells_z), jnp.float32)
        near[:, pl.ds(0, LAG_MAX)] = jnp.zeros((2, LAG_MAX, cells_y, cells_z), jnp.float32)
        far_low[...] = jnp.zeros((2, LAG_MAX, cells_y, cells_z), jnp.float32)

    @pl.when(jnp.logical_not(has_upper))
    def _():
        wide0[:, pl.ds(RIM + extent, RIM)] = jnp.zeros((2, RIM, cells_y, cells_z), jnp.float32)
        wide1[:, pl.ds(RIM + extent, RIM)] = jnp.zeros((2, RIM, cells_y, cells_z), jnp.float32)
        near[:, pl.ds(LAG_MAX + extent, LAG_MAX)] = jnp.zeros((2, LAG_MAX, cells_y, cells_z), jnp.float32)
        far_high[...] = jnp.zeros((2, LAG_MAX, cells_y, cells_z), jnp.float32)

    pl.semaphore_wait(barrier, has_lower.astype(jnp.int32) + has_upper.astype(jnp.int32))

    start(first)

    padded[:, :, pl.ds(0, LEFT_PAD)] = jnp.zeros((2, extent, LEFT_PAD, cells_z), jnp.float32)
    padded[:, :, pl.ds(LEFT_PAD + cells_y, LEFT_PAD)] = jnp.zeros((2, extent, LEFT_PAD, cells_z), jnp.float32)
    for one in small:
        one.wait()

    rows = extent * cells_y
    for f, (place_x, place_y, pulse) in enumerate(((source_x, source_y, source_t), (record_x, record_y, record_t))):
        number = place_x.shape[1]
        cell = (place_x[...] - me * extent) * cells_y + place_y[...]
        hits = jnp.where(lax.broadcasted_iota(jnp.int32, (rows, number), 0) == cell, 1.0, 0.0).astype(jnp.bfloat16)
        line = lax.broadcasted_iota(jnp.int32, (STEPS * cells_z, number), 0)
        spread = jnp.zeros((STEPS * cells_z, number), jnp.float32)
        for moment in range(STEPS):
            spread = jnp.where(line == moment * cells_z + depths[f], pulse[pl.ds(moment, 1), :], spread)
        plane = jnp.zeros((rows, STEPS * cells_z), jnp.float32)
        for part in split_halves(spread):
            plane = plane + lax.dot_general(hits, part, (((1,), (1,)), ((), ())), preferred_element_type=jnp.float32)
        for moment in range(STEPS):
            added[moment, f] = plane[:, moment * cells_z : (moment + 1) * cells_z].reshape(extent, cells_y, cells_z)

    band = depth_band(cells_z)

    def beside(moment, wide, before, begin, end):
        for f in range(2):
            flat = wide[f, pl.ds(RIM + begin, end - begin)].reshape((end - begin) * cells_y, cells_z)
            high, low = split_halves(flat)
            along = jnp.dot(jnp.concatenate([high, low, high], axis=1), band, preferred_element_type=jnp.float32)
            along = along.reshape(end - begin, cells_y, cells_z)
            for x in range(begin, end, RIM):
                centre = wide[f, pl.ds(RIM + x, RIM)]
                total = 3.0 * stencil[0] * centre + along[x - begin : x - begin + RIM]
                for distance in range(1, 5):
                    pair = padded[f, pl.ds(x, RIM), pl.ds(LEFT_PAD - distance, cells_y)] + padded[f, pl.ds(x, RIM), pl.ds(LEFT_PAD + distance, cells_y)]
                    total = total + stencil[distance] * pair
                partial[f, pl.ds(x, RIM)] = (
                    2.0 * centre - before(f, x) + velocity[pl.ds(x, RIM)] * total + added[moment, f, pl.ds(x, RIM)]
                )

    def finished(wide, f, x):
        total = None
        for distance in range(1, 5):
            pair = wide[f, pl.ds(RIM + x - distance, RIM)] + wide[f, pl.ds(RIM + x + distance, RIM)]
            term = stencil[distance] * pair
            total = term if total is None else total + term
        return partial[f, pl.ds(x, RIM)] + velocity[pl.ds(x, RIM)] * total

    inner = range(RIM, extent - RIM, RIM)
    edges = (0, extent - RIM)

    def keep_first(f, x):
        value = finished(wide0, f, x)
        wide1[f, pl.ds(RIM + x, RIM)] = value
        padded[f, pl.ds(x, RIM), pl.ds(LEFT_PAD, cells_y)] = value

    def keep_final(f, x):
        value = finished(wide1, f, x)
        near[f, pl.ds(LAG_MAX + x, RIM)] = value
        squares[f, pl.ds(REACH + x, RIM)] = value * value

    for one in large:
        one.wait()
    beside(0, wide0, lambda f, x: prior[f, pl.ds(x, RIM)], 0, extent)
    for f in range(2):
        for x in inner:
            keep_first(f, x)
    arrive(first)
    for f in range(2):
        for x in edges:
            keep_first(f, x)
    start(second)

    def earlier(f, x):
        return wide0[f, pl.ds(RIM + x, RIM)]

    beside(1, wide1, earlier, RIM, extent - RIM)
    for f in range(2):
        for x in inner:
            keep_final(f, x)
    start(near_early)
    start(far_early)
    for x in edges:
        beside(1, wide1, earlier, x, x + RIM)
    arrive(second)
    for f in range(2):
        for x in edges:
            keep_final(f, x)
    start(near_late)
    start(far_late)

    signed = lax.broadcasted_iota(jnp.int32, (2 * LAG_MAX + 1, lags), 0) - LAG_MAX
    same = jnp.where(signed == offsets_row[...], 1.0, 0.0)
    tally = jnp.sum(same, axis=1, keepdims=True)
    signed_column = lax.broadcasted_iota(jnp.int32, (2 * LAG_MAX + 1, cells_z), 0) - LAG_MAX
    weight = (signed_column * signed_column).astype(jnp.float32) / (LAG_MAX * LAG_MAX * lags)
    weights[pl.ds(0, 2 * LAG_MAX + 1), :] = weight * tally

    step = 2

    def gather(inside, first, last):
        for f, out in ((0, adjoint_source), (1, adjoint_record)):
            sign = 2 if f == 0 else -2
            for x in range(0, extent, step):
                total = None if first else partial[f, pl.ds(x, step)]
                for lag in range(-LAG_MAX, LAG_MAX + 1):
                    place = x + sign * lag
                    if lag == 0 or not inside(place):
                        continue
                    term = weights[pl.ds(lag + LAG_MAX, 1), :] * squares[1 - f, pl.ds(REACH + place, step)]
                    total = term if total is None else total + term
                if last:
                    out[pl.ds(x, step)] = near[f, pl.ds(LAG_MAX + x, step)] * total
                else:
                    partial[f, pl.ds(x, step)] = total

    gather(lambda place: 0 <= place < extent, True, False)

    arrive(near_early)
    arrive(near_late)

    def picture(k, carry):
        shift = offsets[k]
        left = near[0, pl.ds(LAG_MAX - shift, extent)]
        right = near[1, pl.ds(LAG_MAX + shift, extent)]
        images[k] = (left * right).astype(jnp.bfloat16)
        return carry

    lax.fori_loop(0, lags, picture, 0)

    for f in range(2):
        for side in (0, LAG_MAX + extent):
            value = near[f, pl.ds(side, LAG_MAX)]
            squares[f, pl.ds(REACH - LAG_MAX + side, LAG_MAX)] = value * value

    def close(place):
        return -LAG_MAX <= place < extent + LAG_MAX

    gather(lambda place: close(place) and not 0 <= place < extent, False, False)

    arrive(far_early)
    arrive(far_late)
    for f in range(2):
        for far, side in ((far_low, 0), (far_high, REACH + extent + LAG_MAX)):
            value = far[f]
            squares[f, pl.ds(side, LAG_MAX)] = value * value
    gather(lambda place: not close(place), False, True)

    for group in (first, second, near_early, far_early, near_late, far_late):
        leave(group)


def write_out(images, source, record, images_out, source_out, record_out, done):
    lags = images.shape[0]
    copies = [pltpu.make_async_copy(images.at[k], images_out.at[k], done.at[k]) for k in range(lags)]
    copies.append(pltpu.make_async_copy(source, source_out, done.at[lags]))
    copies.append(pltpu.make_async_copy(record, record_out, done.at[lags + 1]))
    for one in copies:
        one.start()
    for one in copies:
        one.wait()


def per_device(
    velocity,
    source_prior,
    source_now,
    record_prior,
    record_now,
    source_inline,
    source_crossline,
    source_pulse,
    receiver_inline,
    receiver_crossline,
    receiver_trace,
    offsets,
):
    extent, cells_y, cells_z = velocity.shape
    lags = offsets.shape[0]
    field = jax.ShapeDtypeStruct(velocity.shape, jnp.float32)
    vmem = pl.BlockSpec(memory_space=pltpu.VMEM)
    hbm = pl.BlockSpec(memory_space=pltpu.HBM)
    shapes = (jax.ShapeDtypeStruct((lags,) + velocity.shape, jnp.bfloat16), field, field)
    sources, receivers = source_inline.shape[0], receiver_inline.shape[0]
    call = pl.pallas_call(
        functools.partial(kernel, lax.axis_size("gx")),
        out_shape=shapes,
        in_specs=[hbm] * 13,
        out_specs=(vmem, vmem, vmem),
        scratch_shapes=[
            pltpu.VMEM((2, extent + 2 * RIM, cells_y, cells_z), jnp.float32),
            pltpu.VMEM((2, extent + 2 * RIM, cells_y, cells_z), jnp.float32),
            pltpu.VMEM((2, extent + 2 * LAG_MAX, cells_y, cells_z), jnp.float32),
            pltpu.VMEM((2, LAG_MAX, cells_y, cells_z), jnp.float32),
            pltpu.VMEM((2, LAG_MAX, cells_y, cells_z), jnp.float32),
            pltpu.VMEM((2, extent, cells_y + 2 * LEFT_PAD, cells_z), jnp.float32),
            pltpu.VMEM((2, extent, cells_y, cells_z), jnp.float32),
            pltpu.VMEM((STEPS, 2, extent, cells_y, cells_z), jnp.float32),
            pltpu.VMEM((2, extent + 2 * REACH, cells_y, cells_z), jnp.float32),
            pltpu.VMEM((2 * LAG_MAX + 8, cells_z), jnp.float32),
            pltpu.SemaphoreType.DMA((4,)),
            pltpu.SemaphoreType.DMA((4,)),
            pltpu.SemaphoreType.DMA((2,)),
            pltpu.SemaphoreType.DMA((2,)),
            pltpu.SemaphoreType.DMA((8,)),
            pltpu.SemaphoreType.DMA((8,)),
            pltpu.VMEM(velocity.shape, jnp.float32),
            pltpu.VMEM((2,) + velocity.shape, jnp.float32),
            pltpu.VMEM((1, sources), jnp.int32),
            pltpu.VMEM((1, sources), jnp.int32),
            pltpu.VMEM((STEPS, sources), jnp.float32),
            pltpu.VMEM((1, receivers), jnp.int32),
            pltpu.VMEM((1, receivers), jnp.int32),
            pltpu.VMEM((STEPS, receivers), jnp.float32),
            pltpu.VMEM((1, lags), jnp.int32),
            pltpu.SMEM((lags,), jnp.int32),
            pltpu.SemaphoreType.DMA((15,)),
        ],
        compiler_params=pltpu.CompilerParams(
            collective_id=0, has_side_effects=True, vmem_limit_bytes=40 * 1024 * 1024
        ),
    )
    operands = (
        velocity,
        source_prior,
        source_now,
        record_prior,
        record_now,
        source_inline.reshape(1, -1),
        source_crossline.reshape(1, -1),
        source_pulse.T,
        receiver_inline.reshape(1, -1),
        receiver_crossline.reshape(1, -1),
        receiver_trace.T,
        offsets.reshape(1, -1),
        offsets,
    )
    held = call(*[pltpu.with_memory_space_constraint(one, pltpu.HBM) for one in operands])
    return pl.pallas_call(
        write_out,
        out_shape=shapes,
        in_specs=[vmem] * len(shapes),
        out_specs=(hbm,) * len(shapes),
        scratch_shapes=[pltpu.SemaphoreType.DMA((lags + 2,))],
        compiler_params=pltpu.CompilerParams(vmem_limit_bytes=4 * 1024 * 1024),
    )(*held)


def solution(mesh):
    in_specs = (
        P("gx", None, None),
        P(("shots", "gx"), None, None),
        P(("shots", "gx"), None, None),
        P(("shots", "gx"), None, None),
        P(("shots", "gx"), None, None),
        P("shots"),
        P("shots"),
        P("shots", None),
        P("shots"),
        P("shots"),
        P("shots", None),
        P(),
    )
    out_specs = (
        P("shots", "gx", None, None),
        P(("shots", "gx"), None, None),
        P(("shots", "gx"), None, None),
    )
    return jax.shard_map(
        per_device, mesh=mesh, in_specs=in_specs, out_specs=out_specs, check_vma=False
    )
```

```python
import functools

import jax
import jax.numpy as jnp
from jax import lax
from jax.experimental import pallas as pl
from jax.experimental.pallas import tpu as pltpu
from jax.sharding import PartitionSpec as P

STEPS = 2
LAG_MAX = 8
REACH = 2 * LAG_MAX
RIM = 4

stencil = (-205.0 / 72.0, 8.0 / 5.0, -1.0 / 5.0, 8.0 / 315.0, -1.0 / 560.0)
depths = (3, 1)
LEFT_PAD = 8


def split_halves(x):
    high = x.astype(jnp.bfloat16)
    low = (x - high.astype(jnp.float32)).astype(jnp.bfloat16)
    return high, low


def depth_band(cells_z):
    rows = lax.broadcasted_iota(jnp.int32, (cells_z, cells_z), 0)
    columns = lax.broadcasted_iota(jnp.int32, (cells_z, cells_z), 1)
    apart = jnp.abs(rows - columns)
    band = jnp.zeros((cells_z, cells_z), jnp.float32)
    for distance in range(1, 5):
        band = jnp.where(apart == distance, stencil[distance], band)
    high, low = split_halves(band)
    return jnp.concatenate([high, high, low], axis=0)


def kernel(
    count,
    velocity_hbm,
    source_prior,
    source_now,
    record_prior,
    record_now,
    source_x_hbm,
    source_y_hbm,
    source_t_hbm,
    record_x_hbm,
    record_y_hbm,
    record_t_hbm,
    offsets_row_hbm,
    offsets_hbm,
    images,
    adjoint_source,
    adjoint_record,
    wide0,
    wide1,
    near,
    far_low,
    far_high,
    padded,
    partial,
    added,
    squares,
    weights,
    send0,
    recv0,
    send1,
    recv1,
    send2,
    recv2,
    velocity,
    prior,
    source_x,
    source_y,
    source_t,
    record_x,
    record_y,
    record_t,
    offsets_row,
    offsets,
    loaded,
):
    extent, cells_y, cells_z = velocity.shape
    lags = images.shape[0]
    small = [
        pltpu.make_async_copy(src, dst, loaded.at[slot])
        for slot, (src, dst) in enumerate((
            (record_x_hbm, record_x),
            (record_y_hbm, record_y),
            (record_t_hbm, record_t),
            (source_x_hbm, source_x),
            (source_y_hbm, source_y),
            (source_t_hbm, source_t),
            (offsets_row_hbm, offsets_row),
            (offsets_hbm, offsets),
        ))
    ]
    me = lax.axis_index("gx")
    has_lower = me > 0
    has_upper = me < count - 1
    lower = jnp.maximum(me - 1, 0)
    upper = jnp.minimum(me + 1, count - 1)
    nows = (source_now, record_now)
    priors = (source_prior, record_prior)

    def copy(src, dst, send, recv, device):
        return pltpu.make_async_remote_copy(
            src_ref=src,
            dst_ref=dst,
            send_sem=send,
            recv_sem=recv,
            device_id={"gx": device},
            device_id_type=pl.DeviceIdType.MESH,
        )

    down, up = [], []
    for f in range(2):
        down.append(copy(nows[f].at[pl.ds(0, RIM)], wide0.at[f, pl.ds(RIM + extent, RIM)], send0.at[f], recv0.at[f], lower))
        up.append(copy(nows[f].at[pl.ds(extent - RIM, RIM)], wide0.at[f, pl.ds(0, RIM)], send0.at[2 + f], recv0.at[2 + f], upper))
    first = (down, up)
    second = (
        [copy(wide1.at[:, pl.ds(RIM, RIM)], wide1.at[:, pl.ds(RIM + extent, RIM)], send1.at[0], recv1.at[0], lower)],
        [copy(wide1.at[:, pl.ds(extent, RIM)], wide1.at[:, pl.ds(0, RIM)], send1.at[1], recv1.at[1], upper)],
    )

    def final_copies(slot, to_lower, length):
        shared = send2.at[slot], recv2.at[slot]
        opposite = extent - to_lower - length

        def target(first_cell, low_side):
            if low_side:
                if first_cell >= extent - LAG_MAX:
                    return near.at[:, pl.ds(first_cell - extent + LAG_MAX, length)]
                return far_low.at[:, pl.ds(first_cell, length)]
            if first_cell < LAG_MAX:
                return near.at[:, pl.ds(LAG_MAX + extent + first_cell, length)]
            return far_high.at[:, pl.ds(first_cell - LAG_MAX, length)]

        return (
            [copy(near.at[:, pl.ds(LAG_MAX + to_lower, length)], target(to_lower, False), *shared, lower)],
            [copy(near.at[:, pl.ds(LAG_MAX + opposite, length)], target(opposite, True), send2.at[4 + slot], recv2.at[4 + slot], upper)],
        )

    near_early = final_copies(0, RIM, LAG_MAX - RIM)
    far_early = final_copies(1, LAG_MAX, extent - RIM - LAG_MAX)
    near_late = final_copies(2, 0, RIM)
    far_late = final_copies(3, extent - RIM, RIM)

    def start(group):
        @pl.when(has_lower)
        def _():
            for one in group[0]:
                one.start()

        @pl.when(has_upper)
        def _():
            for one in group[1]:
                one.start()

    def arrive(group):
        @pl.when(has_upper)
        def _():
            for one in group[0]:
                one.wait_recv()

        @pl.when(has_lower)
        def _():
            for one in group[1]:
                one.wait_recv()

    def leave(group):
        @pl.when(has_lower)
        def _():
            for one in group[0]:
                one.wait_send()

        @pl.when(has_upper)
        def _():
            for one in group[1]:
                one.wait_send()

    large = []
    for f in range(2):
        large.append((nows[f], wide0.at[f, pl.ds(RIM, extent)]))
        large.append((nows[f], padded.at[f, :, pl.ds(LEFT_PAD, cells_y)]))
        large.append((priors[f], prior.at[f]))
    large.append((velocity_hbm, velocity))
    large = [
        pltpu.make_async_copy(src, dst, loaded.at[len(small) + slot])
        for slot, (src, dst) in enumerate(large)
    ]

    barrier = pltpu.get_barrier_semaphore()

    @pl.when(has_lower)
    def _():
        pl.semaphore_signal(barrier, inc=1, device_id={"gx": lower}, device_id_type=pl.DeviceIdType.MESH)

    @pl.when(has_upper)
    def _():
        pl.semaphore_signal(barrier, inc=1, device_id={"gx": upper}, device_id_type=pl.DeviceIdType.MESH)

    for one in small + large:
        one.start()

    @pl.when(jnp.logical_not(has_lower))
    def _():
        wide0[:, pl.ds(0, RIM)] = jnp.zeros((2, RIM, cells_y, cells_z), jnp.float32)
        wide1[:, pl.ds(0, RIM)] = jnp.zeros((2, RIM, cells_y, cells_z), jnp.float32)
        near[:, pl.ds(0, LAG_MAX)] = jnp.zeros((2, LAG_MAX, cells_y, cells_z), jnp.float32)
        far_low[...] = jnp.zeros((2, LAG_MAX, cells_y, cells_z), jnp.float32)

    @pl.when(jnp.logical_not(has_upper))
    def _():
        wide0[:, pl.ds(RIM + extent, RIM)] = jnp.zeros((2, RIM, cells_y, cells_z), jnp.float32)
        wide1[:, pl.ds(RIM + extent, RIM)] = jnp.zeros((2, RIM, cells_y, cells_z), jnp.float32)
        near[:, pl.ds(LAG_MAX + extent, LAG_MAX)] = jnp.zeros((2, LAG_MAX, cells_y, cells_z), jnp.float32)
        far_high[...] = jnp.zeros((2, LAG_MAX, cells_y, cells_z), jnp.float32)

    pl.semaphore_wait(barrier, has_lower.astype(jnp.int32) + has_upper.astype(jnp.int32))

    start(first)

    padded[:, :, pl.ds(0, LEFT_PAD)] = jnp.zeros((2, extent, LEFT_PAD, cells_z), jnp.float32)
    padded[:, :, pl.ds(LEFT_PAD + cells_y, LEFT_PAD)] = jnp.zeros((2, extent, LEFT_PAD, cells_z), jnp.float32)
    for one in small:
        one.wait()

    rows = extent * cells_y
    for f, (place_x, place_y, pulse) in enumerate(((source_x, source_y, source_t), (record_x, record_y, record_t))):
        number = place_x.shape[1]
        cell = (place_x[...] - me * extent) * cells_y + place_y[...]
        hits = jnp.where(lax.broadcasted_iota(jnp.int32, (rows, number), 0) == cell, 1.0, 0.0).astype(jnp.bfloat16)
        line = lax.broadcasted_iota(jnp.int32, (STEPS * cells_z, number), 0)
        spread = jnp.zeros((STEPS * cells_z, number), jnp.float32)
        for moment in range(STEPS):
            spread = jnp.where(line == moment * cells_z + depths[f], pulse[pl.ds(moment, 1), :], spread)
        plane = jnp.zeros((rows, STEPS * cells_z), jnp.float32)
        for part in split_halves(spread):
            plane = plane + lax.dot_general(hits, part, (((1,), (1,)), ((), ())), preferred_element_type=jnp.float32)
        for moment in range(STEPS):
            added[moment, f] = plane[:, moment * cells_z : (moment + 1) * cells_z].reshape(extent, cells_y, cells_z)

    band = depth_band(cells_z)

    def beside(moment, wide, before, begin, end):
        for f in range(2):
            flat = wide[f, pl.ds(RIM + begin, end - begin)].reshape((end - begin) * cells_y, cells_z)
            high, low = split_halves(flat)
            along = jnp.dot(jnp.concatenate([high, low, high], axis=1), band, preferred_element_type=jnp.float32)
            along = along.reshape(end - begin, cells_y, cells_z)
            for x in range(begin, end, RIM):
                centre = wide[f, pl.ds(RIM + x, RIM)]
                total = 3.0 * stencil[0] * centre + along[x - begin : x - begin + RIM]
                for distance in range(1, 5):
                    pair = padded[f, pl.ds(x, RIM), pl.ds(LEFT_PAD - distance, cells_y)] + padded[f, pl.ds(x, RIM), pl.ds(LEFT_PAD + distance, cells_y)]
                    total = total + stencil[distance] * pair
                partial[f, pl.ds(x, RIM)] = (
                    2.0 * centre - before(f, x) + velocity[pl.ds(x, RIM)] * total + added[moment, f, pl.ds(x, RIM)]
                )

    def finished(wide, f, x):
        total = None
        for distance in range(1, 5):
            pair = wide[f, pl.ds(RIM + x - distance, RIM)] + wide[f, pl.ds(RIM + x + distance, RIM)]
            term = stencil[distance] * pair
            total = term if total is None else total + term
        return partial[f, pl.ds(x, RIM)] + velocity[pl.ds(x, RIM)] * total

    inner = range(RIM, extent - RIM, RIM)
    edges = (0, extent - RIM)

    def keep_first(f, x):
        value = finished(wide0, f, x)
        wide1[f, pl.ds(RIM + x, RIM)] = value
        padded[f, pl.ds(x, RIM), pl.ds(LEFT_PAD, cells_y)] = value

    def keep_final(f, x):
        value = finished(wide1, f, x)
        near[f, pl.ds(LAG_MAX + x, RIM)] = value
        squares[f, pl.ds(REACH + x, RIM)] = value * value

    for one in large:
        one.wait()
    def initial(f, x):
        return prior[f, pl.ds(x, RIM)]

    for x in edges:
        beside(0, wide0, initial, x, x + RIM)
    arrive(first)
    for f in range(2):
        for x in edges:
            keep_first(f, x)
    start(second)
    beside(0, wide0, initial, RIM, extent - RIM)
    for f in range(2):
        for x in inner:
            keep_first(f, x)

    def earlier(f, x):
        return wide0[f, pl.ds(RIM + x, RIM)]

    beside(1, wide1, earlier, RIM, extent - RIM)
    for f in range(2):
        for x in inner:
            keep_final(f, x)
    start(near_early)
    start(far_early)
    for x in edges:
        beside(1, wide1, earlier, x, x + RIM)
    arrive(second)
    for f in range(2):
        for x in edges:
            keep_final(f, x)
    start(near_late)
    start(far_late)

    signed = lax.broadcasted_iota(jnp.int32, (2 * LAG_MAX + 1, lags), 0) - LAG_MAX
    same = jnp.where(signed == offsets_row[...], 1.0, 0.0)
    tally = jnp.sum(same, axis=1, keepdims=True)
    signed_column = lax.broadcasted_iota(jnp.int32, (2 * LAG_MAX + 1, cells_z), 0) - LAG_MAX
    weight = (signed_column * signed_column).astype(jnp.float32) / (LAG_MAX * LAG_MAX * lags)
    weights[pl.ds(0, 2 * LAG_MAX + 1), :] = weight * tally

    step = 2

    def gather(inside, first, last):
        for f, out in ((0, adjoint_source), (1, adjoint_record)):
            sign = 2 if f == 0 else -2
            for x in range(0, extent, step):
                total = None if first else partial[f, pl.ds(x, step)]
                for lag in range(-LAG_MAX, LAG_MAX + 1):
                    place = x + sign * lag
                    if lag == 0 or not inside(place):
                        continue
                    term = weights[pl.ds(lag + LAG_MAX, 1), :] * squares[1 - f, pl.ds(REACH + place, step)]
                    total = term if total is None else total + term
                if last:
                    out[pl.ds(x, step)] = near[f, pl.ds(LAG_MAX + x, step)] * total
                else:
                    partial[f, pl.ds(x, step)] = total

    gather(lambda place: 0 <= place < extent, True, False)

    arrive(near_early)
    arrive(near_late)

    def picture(k, carry):
        shift = offsets[k]
        left = near[0, pl.ds(LAG_MAX - shift, extent)]
        right = near[1, pl.ds(LAG_MAX + shift, extent)]
        images[k] = (left * right).astype(jnp.bfloat16)
        return carry

    lax.fori_loop(0, lags, picture, 0)

    for f in range(2):
        for side in (0, LAG_MAX + extent):
            value = near[f, pl.ds(side, LAG_MAX)]
            squares[f, pl.ds(REACH - LAG_MAX + side, LAG_MAX)] = value * value

    def close(place):
        return -LAG_MAX <= place < extent + LAG_MAX

    gather(lambda place: close(place) and not 0 <= place < extent, False, False)

    arrive(far_early)
    arrive(far_late)
    for f in range(2):
        for far, side in ((far_low, 0), (far_high, REACH + extent + LAG_MAX)):
            value = far[f]
            squares[f, pl.ds(side, LAG_MAX)] = value * value
    gather(lambda place: not close(place), False, True)

    for group in (first, second, near_early, far_early, near_late, far_late):
        leave(group)


def write_out(*refs):
    count = (len(refs) - 1) // 2
    copies = [pltpu.make_async_copy(refs[i], refs[count + i], refs[-1].at[i]) for i in range(count)]
    for one in copies:
        one.start()
    for one in copies:
        one.wait()


def per_device(
    velocity,
    source_prior,
    source_now,
    record_prior,
    record_now,
    source_inline,
    source_crossline,
    source_pulse,
    receiver_inline,
    receiver_crossline,
    receiver_trace,
    offsets,
):
    extent, cells_y, cells_z = velocity.shape
    lags = offsets.shape[0]
    field = jax.ShapeDtypeStruct(velocity.shape, jnp.float32)
    vmem = pl.BlockSpec(memory_space=pltpu.VMEM)
    hbm = pl.BlockSpec(memory_space=pltpu.HBM)
    shapes = (jax.ShapeDtypeStruct((lags,) + velocity.shape, jnp.bfloat16), field, field)
    sources, receivers = source_inline.shape[0], receiver_inline.shape[0]
    call = pl.pallas_call(
        functools.partial(kernel, lax.axis_size("gx")),
        out_shape=shapes,
        in_specs=[hbm] * 13,
        out_specs=(vmem, vmem, vmem),
        scratch_shapes=[
            pltpu.VMEM((2, extent + 2 * RIM, cells_y, cells_z), jnp.float32),
            pltpu.VMEM((2, extent + 2 * RIM, cells_y, cells_z), jnp.float32),
            pltpu.VMEM((2, extent + 2 * LAG_MAX, cells_y, cells_z), jnp.float32),
            pltpu.VMEM((2, LAG_MAX, cells_y, cells_z), jnp.float32),
            pltpu.VMEM((2, LAG_MAX, cells_y, cells_z), jnp.float32),
            pltpu.VMEM((2, extent, cells_y + 2 * LEFT_PAD, cells_z), jnp.float32),
            pltpu.VMEM((2, extent, cells_y, cells_z), jnp.float32),
            pltpu.VMEM((STEPS, 2, extent, cells_y, cells_z), jnp.float32),
            pltpu.VMEM((2, extent + 2 * REACH, cells_y, cells_z), jnp.float32),
            pltpu.VMEM((2 * LAG_MAX + 8, cells_z), jnp.float32),
            pltpu.SemaphoreType.DMA((4,)),
            pltpu.SemaphoreType.DMA((4,)),
            pltpu.SemaphoreType.DMA((2,)),
            pltpu.SemaphoreType.DMA((2,)),
            pltpu.SemaphoreType.DMA((8,)),
            pltpu.SemaphoreType.DMA((8,)),
            pltpu.VMEM(velocity.shape, jnp.float32),
            pltpu.VMEM((2,) + velocity.shape, jnp.float32),
            pltpu.VMEM((1, sources), jnp.int32),
            pltpu.VMEM((1, sources), jnp.int32),
            pltpu.VMEM((STEPS, sources), jnp.float32),
            pltpu.VMEM((1, receivers), jnp.int32),
            pltpu.VMEM((1, receivers), jnp.int32),
            pltpu.VMEM((STEPS, receivers), jnp.float32),
            pltpu.VMEM((1, lags), jnp.int32),
            pltpu.SMEM((lags,), jnp.int32),
            pltpu.SemaphoreType.DMA((15,)),
        ],
        compiler_params=pltpu.CompilerParams(
            collective_id=0, has_side_effects=True, vmem_limit_bytes=40 * 1024 * 1024
        ),
    )
    operands = (
        velocity,
        source_prior,
        source_now,
        record_prior,
        record_now,
        source_inline.reshape(1, -1),
        source_crossline.reshape(1, -1),
        source_pulse.T,
        receiver_inline.reshape(1, -1),
        receiver_crossline.reshape(1, -1),
        receiver_trace.T,
        offsets.reshape(1, -1),
        offsets,
    )
    held = call(*[pltpu.with_memory_space_constraint(one, pltpu.HBM) for one in operands])
    return pl.pallas_call(
        write_out,
        out_shape=shapes,
        in_specs=[vmem] * len(shapes),
        out_specs=(hbm,) * len(shapes),
        scratch_shapes=[pltpu.SemaphoreType.DMA((len(shapes),))],
        compiler_params=pltpu.CompilerParams(vmem_limit_bytes=4 * 1024 * 1024),
    )(*held)


def solution(mesh):
    in_specs = (
        P("gx", None, None),
        P(("shots", "gx"), None, None),
        P(("shots", "gx"), None, None),
        P(("shots", "gx"), None, None),
        P(("shots", "gx"), None, None),
        P("shots"),
        P("shots"),
        P("shots", None),
        P("shots"),
        P("shots"),
        P("shots", None),
        P(),
    )
    out_specs = (
        P("shots", "gx", None, None),
        P(("shots", "gx"), None, None),
        P(("shots", "gx"), None, None),
    )
    return jax.shard_map(
        per_device, mesh=mesh, in_specs=in_specs, out_specs=out_specs, check_vma=False
    )
```

```python
import functools

import jax
import jax.numpy as jnp
from jax import lax
from jax.experimental import pallas as pl
from jax.experimental.pallas import tpu as pltpu
from jax.sharding import PartitionSpec as P

STEPS = 2
LAG_MAX = 8
REACH = 2 * LAG_MAX
RIM = 4

stencil = (-205.0 / 72.0, 8.0 / 5.0, -1.0 / 5.0, 8.0 / 315.0, -1.0 / 560.0)
depths = (3, 1)
LEFT_PAD = 8


def split_halves(x):
    high = x.astype(jnp.bfloat16)
    low = (x - high.astype(jnp.float32)).astype(jnp.bfloat16)
    return high, low


def depth_band(cells_z):
    rows = lax.broadcasted_iota(jnp.int32, (cells_z, cells_z), 0)
    columns = lax.broadcasted_iota(jnp.int32, (cells_z, cells_z), 1)
    apart = jnp.abs(rows - columns)
    band = jnp.zeros((cells_z, cells_z), jnp.float32)
    for distance in range(1, 5):
        band = jnp.where(apart == distance, stencil[distance], band)
    high, low = split_halves(band)
    return jnp.concatenate([high, high, low], axis=0)


def kernel(
    count,
    velocity_hbm,
    source_prior,
    source_now,
    record_prior,
    record_now,
    source_x_hbm,
    source_y_hbm,
    source_t_hbm,
    record_x_hbm,
    record_y_hbm,
    record_t_hbm,
    offsets_row_hbm,
    offsets_hbm,
    images,
    adjoint_source,
    adjoint_record,
    wide0,
    wide1,
    near,
    far_low,
    far_high,
    padded,
    partial,
    added,
    squares,
    weights,
    send0,
    recv0,
    send1,
    recv1,
    send2,
    recv2,
    velocity,
    prior,
    source_x,
    source_y,
    source_t,
    record_x,
    record_y,
    record_t,
    offsets_row,
    offsets,
    loaded,
):
    extent, cells_y, cells_z = velocity.shape
    lags = images.shape[0]
    small = [
        pltpu.make_async_copy(src, dst, loaded.at[slot])
        for slot, (src, dst) in enumerate((
            (record_x_hbm, record_x),
            (record_y_hbm, record_y),
            (record_t_hbm, record_t),
            (source_x_hbm, source_x),
            (source_y_hbm, source_y),
            (source_t_hbm, source_t),
            (offsets_row_hbm, offsets_row),
            (offsets_hbm, offsets),
        ))
    ]
    me = lax.axis_index("gx")
    has_lower = me > 0
    has_upper = me < count - 1
    lower = jnp.maximum(me - 1, 0)
    upper = jnp.minimum(me + 1, count - 1)
    nows = (source_now, record_now)
    priors = (source_prior, record_prior)

    def copy(src, dst, send, recv, device):
        return pltpu.make_async_remote_copy(
            src_ref=src,
            dst_ref=dst,
            send_sem=send,
            recv_sem=recv,
            device_id={"gx": device},
            device_id_type=pl.DeviceIdType.MESH,
        )

    down, up = [], []
    for f in range(2):
        down.append(copy(nows[f].at[pl.ds(0, RIM)], wide0.at[f, pl.ds(RIM + extent, RIM)], send0.at[f], recv0.at[f], lower))
        up.append(copy(nows[f].at[pl.ds(extent - RIM, RIM)], wide0.at[f, pl.ds(0, RIM)], send0.at[2 + f], recv0.at[2 + f], upper))
    first = (down, up)
    second = [
        (
            [copy(wide1.at[f, pl.ds(RIM, RIM)], wide1.at[f, pl.ds(RIM + extent, RIM)], send1.at[f], recv1.at[f], lower)],
            [copy(wide1.at[f, pl.ds(extent, RIM)], wide1.at[f, pl.ds(0, RIM)], send1.at[2 + f], recv1.at[2 + f], upper)],
        )
        for f in range(2)
    ]

    def final_copies(slot, to_lower, length):
        shared = send2.at[slot], recv2.at[slot]
        opposite = extent - to_lower - length

        def target(first_cell, low_side):
            if low_side:
                if first_cell >= extent - LAG_MAX:
                    return near.at[:, pl.ds(first_cell - extent + LAG_MAX, length)]
                return far_low.at[:, pl.ds(first_cell, length)]
            if first_cell < LAG_MAX:
                return near.at[:, pl.ds(LAG_MAX + extent + first_cell, length)]
            return far_high.at[:, pl.ds(first_cell - LAG_MAX, length)]

        return (
            [copy(near.at[:, pl.ds(LAG_MAX + to_lower, length)], target(to_lower, False), *shared, lower)],
            [copy(near.at[:, pl.ds(LAG_MAX + opposite, length)], target(opposite, True), send2.at[4 + slot], recv2.at[4 + slot], upper)],
        )

    near_early = final_copies(0, RIM, LAG_MAX - RIM)
    far_early = final_copies(1, LAG_MAX, extent - RIM - LAG_MAX)
    near_late = final_copies(2, 0, RIM)
    far_late = final_copies(3, extent - RIM, RIM)

    def start(group):
        @pl.when(has_lower)
        def _():
            for one in group[0]:
                one.start()

        @pl.when(has_upper)
        def _():
            for one in group[1]:
                one.start()

    def arrive(group):
        @pl.when(has_upper)
        def _():
            for one in group[0]:
                one.wait_recv()

        @pl.when(has_lower)
        def _():
            for one in group[1]:
                one.wait_recv()

    def leave(group):
        @pl.when(has_lower)
        def _():
            for one in group[0]:
                one.wait_send()

        @pl.when(has_upper)
        def _():
            for one in group[1]:
                one.wait_send()

    large = []
    for f in range(2):
        large.append((nows[f], wide0.at[f, pl.ds(RIM, extent)]))
        large.append((nows[f], padded.at[f, :, pl.ds(LEFT_PAD, cells_y)]))
        large.append((priors[f], prior.at[f]))
    large.append((velocity_hbm, velocity))
    large = [
        pltpu.make_async_copy(src, dst, loaded.at[len(small) + slot])
        for slot, (src, dst) in enumerate(large)
    ]

    barrier = pltpu.get_barrier_semaphore()

    @pl.when(has_lower)
    def _():
        pl.semaphore_signal(barrier, inc=1, device_id={"gx": lower}, device_id_type=pl.DeviceIdType.MESH)

    @pl.when(has_upper)
    def _():
        pl.semaphore_signal(barrier, inc=1, device_id={"gx": upper}, device_id_type=pl.DeviceIdType.MESH)

    for one in small + large:
        one.start()

    @pl.when(jnp.logical_not(has_lower))
    def _():
        wide0[:, pl.ds(0, RIM)] = jnp.zeros((2, RIM, cells_y, cells_z), jnp.float32)
        wide1[:, pl.ds(0, RIM)] = jnp.zeros((2, RIM, cells_y, cells_z), jnp.float32)
        near[:, pl.ds(0, LAG_MAX)] = jnp.zeros((2, LAG_MAX, cells_y, cells_z), jnp.float32)
        far_low[...] = jnp.zeros((2, LAG_MAX, cells_y, cells_z), jnp.float32)

    @pl.when(jnp.logical_not(has_upper))
    def _():
        wide0[:, pl.ds(RIM + extent, RIM)] = jnp.zeros((2, RIM, cells_y, cells_z), jnp.float32)
        wide1[:, pl.ds(RIM + extent, RIM)] = jnp.zeros((2, RIM, cells_y, cells_z), jnp.float32)
        near[:, pl.ds(LAG_MAX + extent, LAG_MAX)] = jnp.zeros((2, LAG_MAX, cells_y, cells_z), jnp.float32)
        far_high[...] = jnp.zeros((2, LAG_MAX, cells_y, cells_z), jnp.float32)

    pl.semaphore_wait(barrier, has_lower.astype(jnp.int32) + has_upper.astype(jnp.int32))

    start(first)

    padded[:, :, pl.ds(0, LEFT_PAD)] = jnp.zeros((2, extent, LEFT_PAD, cells_z), jnp.float32)
    padded[:, :, pl.ds(LEFT_PAD + cells_y, LEFT_PAD)] = jnp.zeros((2, extent, LEFT_PAD, cells_z), jnp.float32)
    for one in small:
        one.wait()

    rows = extent * cells_y
    for f, (place_x, place_y, pulse) in enumerate(((source_x, source_y, source_t), (record_x, record_y, record_t))):
        number = place_x.shape[1]
        cell = (place_x[...] - me * extent) * cells_y + place_y[...]
        hits = jnp.where(lax.broadcasted_iota(jnp.int32, (rows, number), 0) == cell, 1.0, 0.0).astype(jnp.bfloat16)
        line = lax.broadcasted_iota(jnp.int32, (STEPS * cells_z, number), 0)
        spread = jnp.zeros((STEPS * cells_z, number), jnp.float32)
        for moment in range(STEPS):
            spread = jnp.where(line == moment * cells_z + depths[f], pulse[pl.ds(moment, 1), :], spread)
        plane = jnp.zeros((rows, STEPS * cells_z), jnp.float32)
        for part in split_halves(spread):
            plane = plane + lax.dot_general(hits, part, (((1,), (1,)), ((), ())), preferred_element_type=jnp.float32)
        for moment in range(STEPS):
            added[moment, f] = plane[:, moment * cells_z : (moment + 1) * cells_z].reshape(extent, cells_y, cells_z)

    band = depth_band(cells_z)

    def beside(moment, wide, before, begin, end):
        for f in range(2):
            flat = wide[f, pl.ds(RIM + begin, end - begin)].reshape((end - begin) * cells_y, cells_z)
            high, low = split_halves(flat)
            along = jnp.dot(jnp.concatenate([high, low, high], axis=1), band, preferred_element_type=jnp.float32)
            along = along.reshape(end - begin, cells_y, cells_z)
            for x in range(begin, end, RIM):
                centre = wide[f, pl.ds(RIM + x, RIM)]
                total = 3.0 * stencil[0] * centre + along[x - begin : x - begin + RIM]
                for distance in range(1, 5):
                    pair = padded[f, pl.ds(x, RIM), pl.ds(LEFT_PAD - distance, cells_y)] + padded[f, pl.ds(x, RIM), pl.ds(LEFT_PAD + distance, cells_y)]
                    total = total + stencil[distance] * pair
                partial[f, pl.ds(x, RIM)] = (
                    2.0 * centre - before(f, x) + velocity[pl.ds(x, RIM)] * total + added[moment, f, pl.ds(x, RIM)]
                )

    def finished(wide, f, x):
        total = None
        for distance in range(1, 5):
            pair = wide[f, pl.ds(RIM + x - distance, RIM)] + wide[f, pl.ds(RIM + x + distance, RIM)]
            term = stencil[distance] * pair
            total = term if total is None else total + term
        return partial[f, pl.ds(x, RIM)] + velocity[pl.ds(x, RIM)] * total

    inner = range(RIM, extent - RIM, RIM)
    edges = (0, extent - RIM)

    def keep_first(f, x):
        value = finished(wide0, f, x)
        wide1[f, pl.ds(RIM + x, RIM)] = value
        padded[f, pl.ds(x, RIM), pl.ds(LEFT_PAD, cells_y)] = value

    def keep_final(f, x):
        value = finished(wide1, f, x)
        near[f, pl.ds(LAG_MAX + x, RIM)] = value
        squares[f, pl.ds(REACH + x, RIM)] = value * value

    for one in large:
        one.wait()
    def initial(f, x):
        return prior[f, pl.ds(x, RIM)]

    for x in edges:
        beside(0, wide0, initial, x, x + RIM)
    arrive(first)
    for f in range(2):
        for x in edges:
            keep_first(f, x)
        start(second[f])
    beside(0, wide0, initial, RIM, extent - RIM)
    for f in range(2):
        for x in inner:
            keep_first(f, x)

    def earlier(f, x):
        return wide0[f, pl.ds(RIM + x, RIM)]

    beside(1, wide1, earlier, RIM, extent - RIM)
    for f in range(2):
        for x in inner:
            keep_final(f, x)
    start(near_early)
    start(far_early)
    for x in edges:
        beside(1, wide1, earlier, x, x + RIM)
    for f in range(2):
        arrive(second[f])
        for x in edges:
            keep_final(f, x)
    start(near_late)
    start(far_late)

    signed = lax.broadcasted_iota(jnp.int32, (2 * LAG_MAX + 1, lags), 0) - LAG_MAX
    same = jnp.where(signed == offsets_row[...], 1.0, 0.0)
    tally = jnp.sum(same, axis=1, keepdims=True)
    signed_column = lax.broadcasted_iota(jnp.int32, (2 * LAG_MAX + 1, cells_z), 0) - LAG_MAX
    weight = (signed_column * signed_column).astype(jnp.float32) / (LAG_MAX * LAG_MAX * lags)
    weights[pl.ds(0, 2 * LAG_MAX + 1), :] = weight * tally

    step = 2

    def gather(inside, first, last):
        for f, out in ((0, adjoint_source), (1, adjoint_record)):
            sign = 2 if f == 0 else -2
            for x in range(0, extent, step):
                total = None if first else partial[f, pl.ds(x, step)]
                for lag in range(-LAG_MAX, LAG_MAX + 1):
                    place = x + sign * lag
                    if lag == 0 or not inside(place):
                        continue
                    term = weights[pl.ds(lag + LAG_MAX, 1), :] * squares[1 - f, pl.ds(REACH + place, step)]
                    total = term if total is None else total + term
                if last:
                    out[pl.ds(x, step)] = near[f, pl.ds(LAG_MAX + x, step)] * total
                else:
                    partial[f, pl.ds(x, step)] = total

    gather(lambda place: 0 <= place < extent, True, False)

    arrive(near_early)
    arrive(near_late)

    def picture(k, carry):
        shift = offsets[k]
        left = near[0, pl.ds(LAG_MAX - shift, extent)]
        right = near[1, pl.ds(LAG_MAX + shift, extent)]
        images[k] = (left * right).astype(jnp.bfloat16)
        return carry

    lax.fori_loop(0, lags, picture, 0)

    for f in range(2):
        for side in (0, LAG_MAX + extent):
            value = near[f, pl.ds(side, LAG_MAX)]
            squares[f, pl.ds(REACH - LAG_MAX + side, LAG_MAX)] = value * value

    def close(place):
        return -LAG_MAX <= place < extent + LAG_MAX

    gather(lambda place: close(place) and not 0 <= place < extent, False, False)

    def middle(place):
        return -LAG_MAX - RIM <= place < extent + LAG_MAX + RIM

    def square_far(low, high):
        for f in range(2):
            value = far_low[f, pl.ds(low, RIM)]
            squares[f, pl.ds(low, RIM)] = value * value
            value = far_high[f, pl.ds(high, RIM)]
            squares[f, pl.ds(REACH + extent + LAG_MAX + high, RIM)] = value * value

    arrive(far_early)
    square_far(LAG_MAX - RIM, 0)
    gather(lambda place: middle(place) and not close(place), False, False)
    arrive(far_late)
    square_far(0, LAG_MAX - RIM)
    gather(lambda place: not middle(place), False, True)

    for group in (first, *second, near_early, far_early, near_late, far_late):
        leave(group)


def write_out(*refs):
    count = (len(refs) - 1) // 2
    copies = [pltpu.make_async_copy(refs[i], refs[count + i], refs[-1].at[i]) for i in range(count)]
    for one in copies:
        one.start()
    for one in copies:
        one.wait()


def per_device(
    velocity,
    source_prior,
    source_now,
    record_prior,
    record_now,
    source_inline,
    source_crossline,
    source_pulse,
    receiver_inline,
    receiver_crossline,
    receiver_trace,
    offsets,
):
    extent, cells_y, cells_z = velocity.shape
    lags = offsets.shape[0]
    field = jax.ShapeDtypeStruct(velocity.shape, jnp.float32)
    vmem = pl.BlockSpec(memory_space=pltpu.VMEM)
    hbm = pl.BlockSpec(memory_space=pltpu.HBM)
    shapes = (jax.ShapeDtypeStruct((lags,) + velocity.shape, jnp.bfloat16), field, field)
    sources, receivers = source_inline.shape[0], receiver_inline.shape[0]
    call = pl.pallas_call(
        functools.partial(kernel, lax.axis_size("gx")),
        out_shape=shapes,
        in_specs=[hbm] * 13,
        out_specs=(vmem, vmem, vmem),
        scratch_shapes=[
            pltpu.VMEM((2, extent + 2 * RIM, cells_y, cells_z), jnp.float32),
            pltpu.VMEM((2, extent + 2 * RIM, cells_y, cells_z), jnp.float32),
            pltpu.VMEM((2, extent + 2 * LAG_MAX, cells_y, cells_z), jnp.float32),
            pltpu.VMEM((2, LAG_MAX, cells_y, cells_z), jnp.float32),
            pltpu.VMEM((2, LAG_MAX, cells_y, cells_z), jnp.float32),
            pltpu.VMEM((2, extent, cells_y + 2 * LEFT_PAD, cells_z), jnp.float32),
            pltpu.VMEM((2, extent, cells_y, cells_z), jnp.float32),
            pltpu.VMEM((STEPS, 2, extent, cells_y, cells_z), jnp.float32),
            pltpu.VMEM((2, extent + 2 * REACH, cells_y, cells_z), jnp.float32),
            pltpu.VMEM((2 * LAG_MAX + 8, cells_z), jnp.float32),
            pltpu.SemaphoreType.DMA((4,)),
            pltpu.SemaphoreType.DMA((4,)),
            pltpu.SemaphoreType.DMA((4,)),
            pltpu.SemaphoreType.DMA((4,)),
            pltpu.SemaphoreType.DMA((8,)),
            pltpu.SemaphoreType.DMA((8,)),
            pltpu.VMEM(velocity.shape, jnp.float32),
            pltpu.VMEM((2,) + velocity.shape, jnp.float32),
            pltpu.VMEM((1, sources), jnp.int32),
            pltpu.VMEM((1, sources), jnp.int32),
            pltpu.VMEM((STEPS, sources), jnp.float32),
            pltpu.VMEM((1, receivers), jnp.int32),
            pltpu.VMEM((1, receivers), jnp.int32),
            pltpu.VMEM((STEPS, receivers), jnp.float32),
            pltpu.VMEM((1, lags), jnp.int32),
            pltpu.SMEM((lags,), jnp.int32),
            pltpu.SemaphoreType.DMA((15,)),
        ],
        compiler_params=pltpu.CompilerParams(
            collective_id=0, has_side_effects=True, vmem_limit_bytes=40 * 1024 * 1024
        ),
    )
    operands = (
        velocity,
        source_prior,
        source_now,
        record_prior,
        record_now,
        source_inline.reshape(1, -1),
        source_crossline.reshape(1, -1),
        source_pulse.T,
        receiver_inline.reshape(1, -1),
        receiver_crossline.reshape(1, -1),
        receiver_trace.T,
        offsets.reshape(1, -1),
        offsets,
    )
    held = call(*[pltpu.with_memory_space_constraint(one, pltpu.HBM) for one in operands])
    return pl.pallas_call(
        write_out,
        out_shape=shapes,
        in_specs=[vmem] * len(shapes),
        out_specs=(hbm,) * len(shapes),
        scratch_shapes=[pltpu.SemaphoreType.DMA((len(shapes),))],
        compiler_params=pltpu.CompilerParams(vmem_limit_bytes=4 * 1024 * 1024),
    )(*held)


def solution(mesh):
    in_specs = (
        P("gx", None, None),
        P(("shots", "gx"), None, None),
        P(("shots", "gx"), None, None),
        P(("shots", "gx"), None, None),
        P(("shots", "gx"), None, None),
        P("shots"),
        P("shots"),
        P("shots", None),
        P("shots"),
        P("shots"),
        P("shots", None),
        P(),
    )
    out_specs = (
        P("shots", "gx", None, None),
        P(("shots", "gx"), None, None),
        P(("shots", "gx"), None, None),
    )
    return jax.shard_map(
        per_device, mesh=mesh, in_specs=in_specs, out_specs=out_specs, check_vma=False
    )
```
